128 devices in a mesh: ctx: 16 (over x_hi, y, core), shard: 8 (over z, x_lo).
Axes of the slice: x: 4 (x_hi: 2, x_lo: 2; x = x_hi * 2 + x_lo), y: 4, z: 4, core: 2. Of those that a mesh axis runs over, the one named last changes fastest.
Arguments:
- inputs: bfloat16 [8, 2048, 768], P('shard', 'ctx'), may hold values from -6 to 6
- cotangent: bfloat16 [8, 2048, 768], P('shard', 'ctx'), may hold values from -6 to 6
- attention_in: float32 [768, 2304], P('shard'), may hold values from -0.21875 to 0.21875
- attention_out: float32 [768, 768], P('shard'), may hold values from -1.25 to 1.25
- expand_weight: float32 [768, 3072], P('shard'), may hold values from -0.21875 to 0.21875
- contract_weight: float32 [3072, 768], P('shard'), may hold values from -0.109375 to 0.109375
- vectors: float32 [12, 768], P(None, 'shard'), may hold values from -0.8 to 1.5, as said below
- first_attention_in: float32 [768, 2304], P('shard'), may hold values from -48 to 48
- first_attention_out: float32 [768, 768], P('shard'), may hold values from -8 to 8
- first_expand_weight: float32 [768, 3072], P('shard'), may hold values from -24 to 24
- first_contract_weight: float32 [3072, 768], P('shard'), may hold values from -56 to 56
- first_vectors: float32 [12, 768], P(None, 'shard'), may hold values from -64 to 64
- second_attention_in: float32 [768, 2304], P('shard'), may hold values from 311.296 to 1245.184
- second_attention_out: float32 [768, 768], P('shard'), may hold values from 9.28 to 36.8
- second_expand_weight: float32 [768, 3072], P('shard'), may hold values from 77.0048 to 311.296
- second_contract_weight: float32 [3072, 768], P('shard'), may hold values from 360.448 to 1458.176
- second_vectors: float32 [12, 768], P(None, 'shard'), may hold values from 425.984 to 1638.4
Outputs:
- layer_output: bfloat16 [8, 2048, 768], P('shard', 'ctx')
- input_grad: float32 [8, 2048, 768], P('shard', 'ctx')
- new_first_attention_in: float32 [768, 2304], P('shard')
- new_second_attention_in: float32 [768, 2304], P('shard')
- new_attention_in: float32 [768, 2304], P('shard')
- new_first_attention_out: float32 [768, 768], P('shard')
- new_second_attention_out: float32 [768, 768], P('shard')
- new_attention_out: float32 [768, 768], P('shard')
- new_first_expand_weight: float32 [768, 3072], P('shard')
- new_second_expand_weight: float32 [768, 3072], P('shard')
- new_expand_weight: float32 [768, 3072], P('shard')
- new_first_contract_weight: float32 [3072, 768], P('shard')
- new_second_contract_weight: float32 [3072, 768], P('shard')
- new_contract_weight: float32 [3072, 768], P('shard')
- new_first_vectors: float32 [12, 768], P(None, 'shard')
- new_second_vectors: float32 [12, 768], P(None, 'shard')
- new_vectors: float32 [12, 768], P(None, 'shard')
The draws below stay inside these ranges and needn't reach their ends.
Inputs may be any that keep to these rules, and one draw needn't show every extreme that they name: `vectors`: rows 0 and 5 (the norms' gains) lie between 0.5 and 1.5; the other rows lie between -0.8 and 0.8.
All inputs are finite; a program needn't handle non-finite values.
Results may differ from the reference program's by a relative error of at most 0.033.
Values may be sent and summed in bfloat16 or wider, within the bound.
A program may use at most 192 MiB of HBM per device.

```python
import math
import jax
import jax.numpy as jnp
from jax import lax

D = 768
FF = 3072
HEAD = 64
STEP = 10
VROWS = 12
LENGTH = 2048
SEQS = 8
TOKENS = 16384


def draw_vectors(key, part):
    key = jax.random.fold_in(key, 11)
    gain_key, bias_key = jax.random.split(key)
    row_total = 8 + FF // D
    gains = jax.random.uniform(gain_key, (row_total, D), jnp.float32, 0.5, 1.5)
    biases = jnp.clip(0.2 * jax.random.normal(bias_key, (row_total, D), jnp.float32), -0.8, 0.8)
    which = jnp.arange(row_total)[:, None]
    is_gain = (which == 0) | (which == 5)
    return jnp.where(is_gain, gains, biases)


def shard_levels(rng, dims, cuts, smallest, top_value):
    level, own = 1.0, jax.random.fold_in(rng, 6)
    for axis_at, parts in cuts:
        steps = jnp.exp(jax.random.uniform(jax.random.fold_in(own, axis_at), (parts,), jnp.float32, smallest / len(cuts), top_value / len(cuts)))
        level = level * jnp.repeat(steps, dims[axis_at] // parts).reshape([-1 if axis == axis_at else 1 for axis in range(len(dims))])
    return level


def gaussian(rng, shape, spread, most, cuts=(), held_as=jnp.bfloat16):
    factor_of = shard_levels(rng, shape, cuts, -0.22, 0.18) if cuts else 1.0
    values = jax.random.normal(rng, shape, jnp.float32) * spread * factor_of
    return jnp.minimum(jnp.maximum(values, -most), most).astype(held_as)


def setup_inputs(seed: int = 0) -> dict:
    arg_keys = jax.random.split(jax.random.key(seed), 18)
    inputs = gaussian(arg_keys[0], (SEQS, LENGTH, D), 1.0, 6.0, ((0, 8), (1, 16)))
    cotangent = gaussian(arg_keys[1], (SEQS, LENGTH, D), 1.0, 6.0, ((0, 8), (1, 16)))
    attention_in = gaussian(arg_keys[2], (D, 3 * D), D ** -0.5, 0.21875, ((0, 8),), jnp.float32)
    attention_out = gaussian(arg_keys[3], (D, D), (max(4, D * 64 // LENGTH)) ** -0.5, 1.25, ((0, 8),), jnp.float32)
    expand_weight = gaussian(arg_keys[4], (D, FF), D ** -0.5, 0.21875, ((0, 8),), jnp.float32)
    contract_weight = gaussian(arg_keys[5], (FF, D), FF ** -0.5, 0.109375, ((0, 8),), jnp.float32)
    vectors = draw_vectors(jax.random.fold_in(arg_keys[17], 71), 0)
    first_attention_in = gaussian(arg_keys[7], (D, 3 * D), (0.067 * TOKENS ** 0.5), 48.0, ((0, 8),), jnp.float32)
    first_attention_out = gaussian(arg_keys[8], (D, D), (0.52 * SEQS ** 0.5), 8.0, ((0, 8),), jnp.float32)
    first_expand_weight = gaussian(arg_keys[9], (D, FF), (0.033 * TOKENS ** 0.5), 24.0, ((0, 8),), jnp.float32)
    first_contract_weight = gaussian(arg_keys[10], (FF, D), (0.072 * TOKENS ** 0.5), 56.0, ((0, 8),), jnp.float32)
    first_vectors = gaussian(arg_keys[11], (VROWS, D), (0.078 * TOKENS ** 0.5), 64.0, ((1, 8),), jnp.float32)
    second_attention_in = jnp.clip(jnp.exp(math.log(1245.184) - 1.3862944 * jax.random.uniform(arg_keys[12], (D, 3 * D), jnp.float32) ** shard_levels(arg_keys[12], (D, 3 * D), ((0, 8),), -0.2, 0.2)), 311.296, 1245.184)
    second_attention_out = jnp.clip(jnp.exp(math.log(36.8) - 1.3776363 * jax.random.uniform(arg_keys[13], (D, D), jnp.float32) ** shard_levels(arg_keys[13], (D, D), ((0, 8),), -0.2, 0.2)), 9.28, 36.8)
    second_expand_weight = jnp.clip(jnp.exp(math.log(311.296) - 1.3968765 * jax.random.uniform(arg_keys[14], (D, FF), jnp.float32) ** shard_levels(arg_keys[14], (D, FF), ((0, 8),), -0.2, 0.2)), 77.0048, 311.296)
    second_contract_weight = jnp.clip(jnp.exp(math.log(1458.176) - 1.397594 * jax.random.uniform(arg_keys[15], (FF, D), jnp.float32) ** shard_levels(arg_keys[15], (FF, D), ((0, 8),), -0.2, 0.2)), 360.448, 1458.176)
    second_vectors = jnp.clip(jnp.exp(math.log(1638.4) - 1.34707364 * jax.random.uniform(arg_keys[16], (VROWS, D), jnp.float32) ** shard_levels(arg_keys[16], (VROWS, D), ((1, 8),), -0.2, 0.2)), 425.984, 1638.4)
    return {"inputs": inputs, "cotangent": cotangent, "attention_in": attention_in, "attention_out": attention_out, "expand_weight": expand_weight, "contract_weight": contract_weight, "vectors": vectors, "first_attention_in": first_attention_in, "first_attention_out": first_attention_out, "first_expand_weight": first_expand_weight, "first_contract_weight": first_contract_weight, "first_vectors": first_vectors, "second_attention_in": second_attention_in, "second_attention_out": second_attention_out, "second_expand_weight": second_expand_weight, "second_contract_weight": second_contract_weight, "second_vectors": second_vectors}


norm_eps = 1e-05
beta_first = 0.9
beta_second = 0.95
adam_eps = 1e-08
decay_matrix = 0.1
rate_matrix = 0.1
rate_vector = 0.5

@jax.custom_vjp
def low(v):
    return lax.optimization_barrier(v.astype(jnp.bfloat16)).astype(jnp.float32)

@jax.custom_vjp
def low_back(v):
    return v

def low_keep(v):
    return (low(v), None)

def low_pass(kept, grad):
    return (grad,)

def back_keep(v):
    return (v, None)

def back_low(kept, grad):
    return (low(grad),)
low.defvjp(low_keep, low_pass)
low_back.defvjp(back_keep, back_low)

def dense_product(left, right):
    return jnp.dot(left, right, preferred_element_type=jnp.float32, precision=lax.Precision.HIGHEST)

def layer_norm(values, scale_row, shift_row):
    average = lax.optimization_barrier(jnp.mean(values, -1, keepdims=True))
    centred = values - average
    variance = lax.optimization_barrier(jnp.mean(centred * centred, -1, keepdims=True))
    return centred * lax.rsqrt(variance + norm_eps) * scale_row + shift_row

def unpack(vector_rows):
    return [vector_rows[position] for position in range(8)] + [vector_rows[8:].reshape(-1)]

def attend(queries, key_rows, value_rows):
    length = queries.shape[0]
    block_size = min(512, length)
    head_count = queries.shape[1] // HEAD
    query_blocks = queries.reshape(length // block_size, block_size, head_count, HEAD)
    key_heads = key_rows.reshape(length, head_count, HEAD)
    value_heads = value_rows.reshape(length, head_count, HEAD)
    starts = jnp.arange(length // block_size, dtype=jnp.int32) * block_size
    key_place = jnp.arange(length, dtype=jnp.int32)

    def one_block(block_args):
        query_block, first_row = block_args
        scores = jnp.einsum('qhd,khd->hqk', query_block, key_heads, precision=lax.Precision.HIGHEST) * HEAD ** (-0.5)
        scores = low_back(scores)
        allowed = key_place[None, :] <= (first_row + jnp.arange(block_size, dtype=jnp.int32))[:, None]
        scores = jnp.where(allowed[None], scores, -1e+30)
        probabilities = low(jax.nn.softmax(scores, axis=-1))
        return jnp.einsum('hqk,khd->qhd', probabilities, value_heads, precision=lax.Precision.HIGHEST)
    outputs = lax.map(jax.checkpoint(one_block), (query_blocks, starts))
    return outputs.reshape(length, head_count * HEAD)

def block_layer(weights, tokens):
    attention_in, attention_out, expand_weight, contract_weight, vectors = [low(weight) for weight in weights]
    model_width = tokens.shape[1]
    gain_one, shift_one, bias_query, bias_value, bias_out, gain_two, shift_two, bias_down, bias_up = unpack(vectors)
    normed = low(layer_norm(tokens, gain_one, shift_one))
    projected = dense_product(normed, attention_in)
    queries = low(low_back(projected[:, :model_width] + bias_query))
    key_rows = low(low_back(projected[:, model_width:2 * model_width]))
    value_rows = low(low_back(projected[:, 2 * model_width:] + bias_value))
    attended = low(low_back(attend(queries, key_rows, value_rows)))
    middle = tokens + low_back(dense_product(attended, attention_out) + bias_out)
    normed_two = low(layer_norm(middle, gain_two, shift_two))
    hidden_pre = low_back(dense_product(normed_two, expand_weight) + bias_up)
    active = low(jax.nn.gelu(hidden_pre, approximate=True))
    return middle + dense_product(active, contract_weight) + bias_down

def adam_step(weight, moment_one, moment_two, gradient, learn_rate, decay_share):
    first_new = beta_first * moment_one + (1.0 - beta_first) * gradient
    second_new = beta_second * moment_two + (1.0 - beta_second) * gradient * gradient
    first_hat = first_new / (1.0 - beta_first ** STEP)
    second_hat = second_new / (1.0 - beta_second ** STEP)
    weight_new = weight - learn_rate * (first_hat / (jnp.sqrt(second_hat) + adam_eps) + decay_share * weight)
    return (first_new, second_new, weight_new)

def reference(inputs, cotangent, attention_in, attention_out, expand_weight, contract_weight, vectors, first_attention_in, first_attention_out, first_expand_weight, first_contract_weight, first_vectors, second_attention_in, second_attention_out, second_expand_weight, second_contract_weight, second_vectors):
    weights = (attention_in, attention_out, expand_weight, contract_weight, vectors)

    def one_sequence(summed, sequence_pair):
        tokens, sequence_cotangent = sequence_pair
        result, pullback = jax.vjp(block_layer, weights, tokens.astype(jnp.float32))
        weight_grads, token_grads = pullback(sequence_cotangent.astype(jnp.float32))
        summed = tuple((before + addend for before, addend in zip(summed, weight_grads)))
        return (summed, (result.astype(jnp.bfloat16), token_grads))
    zero_grads = tuple((jnp.zeros_like(weight) for weight in weights))
    gradients, (layer_output, input_grad) = lax.scan(one_sequence, zero_grads, (inputs, cotangent))
    new_in = adam_step(attention_in, first_attention_in, second_attention_in, gradients[0], rate_matrix, decay_matrix)
    new_out = adam_step(attention_out, first_attention_out, second_attention_out, gradients[1], rate_matrix, decay_matrix)
    new_expand = adam_step(expand_weight, first_expand_weight, second_expand_weight, gradients[2], rate_matrix, decay_matrix)
    new_contract = adam_step(contract_weight, first_contract_weight, second_contract_weight, gradients[3], rate_matrix, decay_matrix)
    new_table = adam_step(vectors, first_vectors, second_vectors, gradients[4], rate_vector, 0.0)
    return (layer_output, input_grad, new_in[0], new_in[1], new_in[2], new_out[0], new_out[1], new_out[2], new_expand[0], new_expand[1], new_expand[2], new_contract[0], new_contract[1], new_contract[2], new_table[0], new_table[1], new_table[2])
```

```python
from functools import partial

import jax
import jax.numpy as jnp
from jax import lax
from jax.experimental import pallas as pl
from jax.experimental.pallas import tpu as pltpu
from jax.sharding import PartitionSpec as P

HEAD = 64
STEP = 10
LANES = 128
GROUP_ROWS = (192, 288)
IN_AT, OUT_AT, VEC_AT = 0, 864, 1440
EXP_AT, CON_AT = 0, 1152
EARLY, OUT_EARLY, VEC_LATE = 2, 192, 672
PART_ROWS = 96
STREAMS = {192: (64, 64, 64), 288: (192, 64, 32), 96: (32, 32, 32)}
MIB = 2**20

norm_eps = 1e-05
beta_first = 0.9
beta_second = 0.95
adam_eps = 1e-08
decay_matrix = 0.1
rate_matrix = 0.1
rate_vector = 0.5

MESH = pl.DeviceIdType.MESH
BF = jnp.bfloat16
F32 = jnp.float32


class Place:
    def __init__(self):
        ctx = lax.axis_index("ctx")
        shard = lax.axis_index("shard")
        self.core = lax.rem(ctx, 2)
        xh, xl = lax.div(ctx, 8), lax.rem(shard, 2)
        self.at = (xh * 2 + xl, lax.rem(lax.div(ctx, 2), 4), lax.div(shard, 2))

    def move(self, axis, by):
        return lax.rem(self.at[axis] + by + 4, 4)

    def device(self, at, core):
        x, y, z = at
        return {
            "ctx": (lax.div(x, 2) * 4 + y) * 2 + core,
            "shard": z * 2 + lax.rem(x, 2),
        }

    def neighbour(self, axis, by):
        at = list(self.at)
        at[axis] = self.move(axis, by)
        return self.device(at, self.core)

    def along(self, axis, by):
        at = list(self.at)
        at[axis] = self.move(axis, by)
        return self.device(at, self.core)

    def of_sequence(self, by_x, by_y, other=0):
        at = (self.move(0, by_x), self.move(1, by_y), self.at[2])
        return self.device(at, 1 - self.core if other else self.core)

    def sibling(self):
        return self.device(self.at, 1 - self.core)


def greet(others):
    barrier = pltpu.get_barrier_semaphore()
    for other in others:
        pl.semaphore_signal(barrier, inc=1, device_id=other, device_id_type=MESH)


def meet(others):
    pl.semaphore_wait(pltpu.get_barrier_semaphore(), len(others))


class Links:
    def __init__(self, send, recv, used=None):
        self.send, self.recv, self.open = send, recv, []
        self.used = [0] if used is None else used

    def branch(self):
        return Links(self.send, self.recv, self.used)

    def take(self, count):
        first = self.used[0]
        self.used[0] += count
        return list(range(first, first + count))

    def copy(self, src, dst, slot, device):
        return pltpu.make_async_remote_copy(
            src_ref=src,
            dst_ref=dst,
            send_sem=self.send.at[slot],
            recv_sem=self.recv.at[slot],
            device_id=device,
            device_id_type=MESH,
        )

    def start(self, src, dst, slot, device):
        made = self.copy(src, dst, slot, device)
        made.start()
        self.open.append(made)

    def arrived(self, dst, slot, device):
        self.copy(dst, dst, slot, device).wait_recv()

    def close(self):
        for made in self.open:
            made.wait_send()
        self.open = []


def step(flows):
    for flow in list(flows):
        try:
            next(flow)
        except StopIteration:
            flows.remove(flow)


def in_step(flows):
    while flows:
        step(flows)


def ring_gather(links, place, axis, block):
    left, right = place.neighbour(axis, -1), place.neighbour(axis, 1)
    s = links.take(6)
    links.start(block(0, 0), block(0, 0), s[0], right)
    links.start(block(0, 1), block(0, 1), s[1], left)
    links.start(block(0, 1), block(0, 1), s[2], right)
    links.start(block(0, 0), block(0, 0), s[3], left)
    yield
    links.arrived(block(-1, 0), s[0], left)
    links.start(block(-1, 0), block(-1, 0), s[4], right)
    links.arrived(block(1, 1), s[1], right)
    links.start(block(1, 1), block(1, 1), s[5], left)
    yield
    links.arrived(block(-1, 1), s[2], left)
    links.arrived(block(1, 0), s[3], right)
    links.arrived(block(2, 0), s[4], left)
    links.arrived(block(2, 1), s[5], right)


def direct_gather(links, place, axis, block):
    s = links.take(3)
    for by in (2, 1, 3):
        links.start(block(0, None), block(0, None), s[by - 1], place.along(axis, by))
    yield
    for by in (1, 3, 2):
        links.arrived(block(-by, None), s[by - 1], place.along(axis, -by))


def ring_reduce(links, place, axis, block, from_left, from_right, got_left, got_right, add, finish):
    left, right = place.neighbour(axis, -1), place.neighbour(axis, 1)
    s = links.take(6)
    links.start(block(2, 0), from_right, s[0], left)
    links.start(block(2, 1), from_left, s[1], right)
    links.start(block(1, 0), got_left(0), s[2], right)
    links.start(block(-1, 1), got_right(1), s[3], left)
    yield
    links.arrived(from_right, s[0], right)
    add(from_right, block(-1, 0))
    links.start(from_right, got_right(0), s[4], left)
    links.arrived(from_left, s[1], left)
    add(from_left, block(1, 1))
    links.start(from_left, got_left(1), s[5], right)
    yield
    links.arrived(got_left(0), s[2], left)
    links.arrived(got_right(1), s[3], right)
    links.arrived(got_right(0), s[4], right)
    links.arrived(got_left(1), s[5], left)
    finish()


def far_exchange(links, place, source, target, over_left, over_right):
    left, right = place.neighbour(0, -1), place.neighbour(0, 1)
    s = links.take(4)
    links.start(source(0), over_left, s[0], right)
    links.start(source(1), over_right, s[1], left)
    yield
    links.arrived(over_left, s[0], left)
    links.start(over_left, target(1, 0), s[2], right)
    links.arrived(over_right, s[1], right)
    links.start(over_right, target(-1, 1), s[3], left)
    yield
    links.arrived(target(0, 0), s[2], left)
    links.arrived(target(0, 1), s[3], right)


def loop_over(sizes, body, index=()):
    if not sizes:
        body(index)
        return

    @pl.loop(0, sizes[0])
    def _(i):
        loop_over(sizes[1:], body, (*index, i))


def add_all(target, *terms):
    lead = target.shape[:-2]
    whole = len(lead) > 0 and lead[-1] * target.shape[-2] * target.shape[-1] <= 4 * 96 * LANES

    def body(index):
        total = terms[0][index].astype(F32)
        for term in terms[1:]:
            total = total + term[index].astype(F32)
        target[index] = total.astype(target.dtype)

    loop_over(lead[:-1] if whole else lead, body)


def add_into(target, term):
    add_all(target, target, term)


def halved(ref, half):
    if half is None:
        return ref
    size = ref.shape[0] // 2
    return ref.at[pl.ds(half * size, size)]


ORDERS = ((0, 1, 2), (1, 2, 0), (2, 0, 1))
LAYOUTS = tuple(order[::-1] for order in ORDERS)


def stream_rows(rows, stream):
    size = STREAMS[rows][stream]
    return pl.ds(sum(STREAMS[rows][:stream]), size)


def stream_buffers(rows):
    return [pltpu.VMEM((4, 4, 4, size, LANES), BF) for size in STREAMS[rows]]


def pieces(refs, stream, free, fixed, half=None):
    index = tuple(fixed[axis] for axis in LAYOUTS[stream] if axis not in free)
    return halved(refs[stream].at[index], half)


def held(ref, stream, outer, free, fixed, half=None):
    index = tuple(fixed[a] for a in LAYOUTS[stream] if a in outer and a not in free)
    return halved(ref.at[index], half)


def places(ref, lead, start, count):
    streams = isinstance(ref, (list, tuple))
    sizes = [r.shape[-2] for r in ref] if streams else [ref.shape[-2]]
    rows = sum(sizes)
    found = []
    while count:
        piece, inner = divmod(start, rows)
        stream = 0
        while inner >= sizes[stream]:
            inner -= sizes[stream]
            stream += 1
        size = min(sizes[stream] - inner, count)
        if streams:
            at = (piece // 4 * 2 + lead[1], piece % 4, lead[0])
            index, target = tuple(at[axis] for axis in LAYOUTS[stream]), ref[stream]
        else:
            index, target = (*lead, piece // 4, piece % 4), ref
        found.append((target, (*index, pl.ds(inner, size)), size))
        start, count = start + size, count - size
    return found


def load_rows(ref, lead, start, count):
    parts = [target[index] for target, index, _ in places(ref, lead, start, count)]
    return parts[0] if len(parts) == 1 else jnp.concatenate(parts, 0)


def store_rows(ref, lead, start, value):
    at = 0
    for target, index, size in places(ref, lead, start, value.shape[0]):
        target[index] = value[at : at + size]
        at += size


def half_of(core, first, second):
    return jnp.where(core == 0, first, second).astype(BF)


def pack_attention(core, inward, outward, table, own):
    for j in range(9):
        at = (j // 3) * 768 + (j % 3) * LANES
        tile = half_of(core, inward[:, at : at + LANES], inward[:, at + 384 : at + 384 + LANES])
        store_rows(own, (), IN_AT + 96 * j, tile)
    for j in range(6):
        tile = outward[:, j * LANES : (j + 1) * LANES].astype(BF)
        store_rows(own, (), OUT_AT + 96 * j, tile)
    wide = jnp.concatenate([table[...], jnp.zeros((12, LANES - 96), F32)], 1)
    store_rows(own, (), VEC_AT, jnp.concatenate([wide, jnp.zeros((4, LANES), F32)], 0).astype(BF))
    store_rows(own, (), VEC_AT + 16, jnp.zeros((80, LANES), BF))


def pack_hidden(core, expand, contract, own):
    for pair in range(4):
        at = pair * 768
        wide = [
            half_of(core, expand[:, at + k : at + k + 192], expand[:, at + k + 192 : at + k + 384])
            for k in (0, 384)
        ]
        wide = jnp.concatenate(wide, 1)
        for j in range(3):
            store_rows(own, (), EXP_AT + 96 * (3 * pair + j), wide[:, j * LANES : (j + 1) * LANES])
    for j in range(6):
        at = slice(j * LANES, (j + 1) * LANES)
        store_rows(own, (), CON_AT + 192 * j, half_of(core, contract[:192, at], contract[192:, at]))


def gather_flow(links, place, out, stream):
    for phase, axis in enumerate(ORDERS[stream]):
        free = ORDERS[stream][:phase]

        def block(offset, half, axis=axis, free=free):
            at = list(place.at)
            at[axis] = place.move(axis, offset)
            return pieces(out, stream, free, at, half)

        yield from (direct_gather if phase < 2 else ring_gather)(links, place, axis, block)


def over_ctx(links, place, first, ref_at, over_left, over_right):
    xh, y = lax.div(place.at[0], 2), place.at[1]

    def by_y(whole):
        def block(offset, half):
            return ref_at(None if whole else xh, place.move(1, offset), half)

        yield from ring_gather(links, place, 1, block)

    def by_x(whole):
        yy = None if whole else y

        def source(half):
            return ref_at(xh, yy, half)

        def target(by, half):
            return ref_at(1 - lax.div(place.move(0, by), 2), yy, half)

        yield from far_exchange(links, place, source, target, over_left, over_right)

    if first == "x":
        yield from by_x(False)
        yield from by_y(True)
    else:
        yield from by_y(False)
        yield from by_x(True)


KV_ROWS = ((0, 160), (160, 96))


def gather_pairs_flow(links, place, out, group, over_left, over_right):
    def at(xh, y, half):
        index = (y, xh) if group == 0 else (xh, y)
        return halved(out.at[tuple(i for i in index if i is not None)], half)

    yield from over_ctx(links, place, "xy"[group], at, over_left, over_right)


def reduce_pairs_flow(links, place, part, out, group, buffers):
    from_left, from_right, got_left, got_right, total, over_left, over_right, far = buffers
    begin, count = KV_ROWS[group]
    xh = lax.div(place.at[0], 2)
    target = out.at[pl.ds(begin, count)]

    def ring(block, finish):
        yield from ring_reduce(
            links, place, 1, block, from_left, from_right,
            lambda half: halved(got_left, half),
            lambda half: halved(got_right, half),
            add_into, finish,
        )

    def exchange(source):
        yield from far_exchange(
            links, place, lambda half: halved(source, half), lambda by, half: halved(far, half),
            over_left, over_right,
        )

    terms = part if group == 0 else total

    def block(offset, half):
        return halved(terms.at[place.move(1, offset)], half)

    if group == 0:
        yield from ring(block, lambda: add_all(total, block(0, None), got_left, got_right))
        yield from exchange(total.at[1 - xh])
        add_all(target, total.at[xh], far)
    else:
        yield from exchange(part.at[1 - xh])
        add_all(total, part.at[xh], far)
        yield from ring(block, lambda: add_all(target, block(0, None), got_left, got_right))


def pairs_scratch(width):
    (_, a), (_, b) = KV_ROWS

    def vmem(*shape):
        return pltpu.VMEM((*shape, width), BF)

    first = [vmem(1, a)] * 2 + [vmem(2, a)] * 3 + [vmem(a // 2)] * 2 + [vmem(a)]
    second = [vmem(b // 2)] * 2 + [vmem(b)] * 2 + [vmem(4, b)] + [vmem(2, b)] * 2 + [vmem(4, b)]
    return first, second


def sum_flow(links, place, part, out, stream, buffers, ring):
    rows = out.shape[-2]
    order = ORDERS[stream]
    term = None
    for phase, axis in enumerate(reversed(order)):
        free = order[: 2 - phase]
        outer = order[: 3 - phase]
        count = 5 if ring and phase == 0 else 4
        mine, buffers = buffers[:count], buffers[count:]
        total = mine[-1]
        if phase == 2:
            at = (place.core, lax.div(place.at[0], 2), place.at[1])
            total = out.at[(*at, stream_rows(rows, stream))]

        def block(offset, half, axis=axis, free=free, outer=outer, term=term):
            at = list(place.at)
            at[axis] = place.move(axis, offset)
            if term is None:
                return pieces(part, stream, free, at, half)
            return held(term, stream, outer, free, at, half)

        if count == 5:
            from_left, from_right, got_left, got_right = mine[:4]

            def finish(block=block, total=total, got_left=got_left, got_right=got_right):
                add_all(total, block(0, None), got_left, got_right)

            yield from ring_reduce(
                links, place, axis, block, from_left, from_right,
                lambda half, got_left=got_left: halved(got_left, half),
                lambda half, got_right=got_right: halved(got_right, half),
                add_into, finish,
            )
        else:
            s = links.take(3)
            for by in (2, 1, 3):
                links.start(block(by, None), mine[by - 1], s[by - 1], place.along(axis, by))
            yield
            for by in (1, 3, 2):
                links.arrived(mine[by - 1], s[by - 1], place.along(axis, -by))
            add_all(total, block(0, None), *mine[:3])
        term = total


def sum_scratch(rows, ring):
    scratch = []
    for size in STREAMS[rows]:
        for phase in range(3):
            lead = (4,) * (2 - phase)
            full = pltpu.VMEM((*lead, size, LANES), BF)
            if ring and phase == 0:
                scratch += [pltpu.VMEM((2, 4, size, LANES), BF)] * 2 + [full] * 3
            else:
                scratch += [full] * 4
    return scratch


def group_flow(links, place, part, out, scratch, ring, at_once):
    count = len(scratch) // 3
    flows = [
        sum_flow(links, place, part, out, s, scratch[count * s : count * (s + 1)], ring)
        for s in range(3)
    ]
    while flows:
        step(flows)
        if flows:
            yield
    yield from (spread_at_once if at_once else spread_flow)(links, place, out)


def spread_at_once(links, place, out):
    core, xh, y = place.core, lax.div(place.at[0], 2), place.at[1]
    mine = out.at[core, xh, y]
    moves = [(bx, by, other) for other in (0, 1) for bx in (0, 2) for by in range(4)][1:]
    s = links.take(15)
    for slot, (bx, by, other) in zip(s, moves):
        links.start(mine, mine, slot, place.of_sequence(bx, by, other))
    yield
    for slot, (bx, by, other) in zip(s, moves):
        theirs = out.at[
            1 - core if other else core, lax.div(place.move(0, -bx), 2), place.move(1, -by)
        ]
        links.arrived(theirs, slot, place.of_sequence(-bx, -by, other))


def spread_flow(links, place, out):
    core, xh, y = place.core, lax.div(place.at[0], 2), place.at[1]
    mine = out.at[core, xh, y]
    moves = [(bx, by) for bx in (0, 2) for by in range(4) if (bx, by) != (0, 0)]
    s = links.take(8)
    for slot, (bx, by) in zip(s, moves):
        links.start(mine, mine, slot, place.of_sequence(bx, by))
    yield
    for slot, (bx, by) in zip(s, moves):
        theirs = out.at[core, lax.div(place.move(0, -bx), 2), place.move(1, -by)]
        links.arrived(theirs, slot, place.of_sequence(-bx, -by))
    links.start(out.at[core], out.at[core], s[7], place.sibling())
    yield
    links.arrived(out.at[1 - core], s[7], place.sibling())


def nt(left, right):
    return lax.dot_general(left, right, (((1,), (1,)), ((), ())), preferred_element_type=F32)


def nn(left, right):
    return jnp.dot(left, right, preferred_element_type=F32)


def causal(core):
    key = lax.broadcasted_iota(jnp.int32, (256, 256), 0)
    query = lax.broadcasted_iota(jnp.int32, (256, 256), 1)
    shift = core * 128
    return lax.rem(key + shift, 256) <= lax.rem(query + shift, 256)


def one_head(tile, which):
    lane = lax.broadcasted_iota(jnp.int32, tile.shape, 1)
    return jnp.where((lane < HEAD) == (which == 0), tile, jnp.zeros_like(tile))


def masked_heads(q_ref, masked):
    for p in range(masked.shape[0] // 2):
        tile = q_ref[:, p * LANES : (p + 1) * LANES] * jnp.asarray(0.125, BF)
        for h in range(2):
            masked[2 * p + h] = one_head(tile, h)


def attend_blocks(p, blocks, allowed, masked, top, mass, acc):
    values = [kv[:, LANES:].T for kv in blocks]
    scores = [[nt(kv[:, :LANES], masked[2 * p + h]) for kv in blocks] for h in range(2)]
    later = []
    for h in range(2):
        head = 2 * p + h
        part = [value[h * HEAD : (h + 1) * HEAD] for value in values]
        if allowed is not None:
            score = jnp.where(allowed, scores[h][0], -1e30)
            high = jnp.max(score, 0, keepdims=True)
            weights = jnp.exp(score - high)
            top[head] = high
            mass[head] = jnp.sum(weights, 0, keepdims=True)
            acc[head] = nn(part[0], weights.astype(BF))
            continue
        old = top[head]
        new = old
        for score in scores[h]:
            new = jnp.maximum(new, jnp.max(score, 0, keepdims=True))
        fade = jnp.exp(old - new)
        top[head] = new
        total, low = mass[head] * fade, []
        for score in scores[h]:
            weight = jnp.exp(score - new)
            total = total + jnp.sum(weight, 0, keepdims=True)
            low.append(weight.astype(BF))
        mass[head] = total
        later.append((head, fade, part, low))
    for head, fade, part, low in later:
        mixed = acc[head] * fade
        for value, weight in zip(part, low):
            mixed = mixed + nn(value, weight)
        acc[head] = mixed


def earlier_blocks(chip, visit, between):
    between(0)

    @pl.loop(0, lax.div(chip, 2))
    def _(j):
        xh, y = lax.div(j, 2), 2 * lax.rem(j, 2)
        visit([(xh, y), (xh, y + 1)])

    between(1)

    @pl.loop(0, lax.rem(chip, 2))
    def _(j):
        visit([(lax.div(chip, 4), 2 * lax.div(lax.rem(chip, 4), 2))])


def read_block(pairs, p, xh, y):
    return jnp.concatenate([pairs[0][p, y, xh], pairs[1][p, xh, y]], 0)


def write_block(pairs, p, xh, y, value):
    cut = KV_ROWS[1][0]
    pairs[0][p, y, xh] = value[:cut]
    pairs[1][p, xh, y] = value[cut:]


def attend_end(p, o_ref, low_ref, top, mass, acc):
    both = jnp.concatenate([acc[2 * p + h] / mass[2 * p + h] for h in range(2)], 0)
    out = both.T
    o_ref[:, p * LANES : (p + 1) * LANES] = out
    low_ref[:, p * LANES : (p + 1) * LANES] = out.astype(BF)
    for head in (2 * p, 2 * p + 1):
        top[head] = top[head] + jnp.log(mass[head])


def attend_back(p, chip, core, pairs, o_ref, go_ref, lse, dq_ref, masked, masked_go, delta, acc, between):
    at = slice(p * LANES, (p + 1) * LANES)
    go = go_ref[:, at]
    product = (go.astype(F32) * o_ref[:, at]).T
    for h in range(2):
        head = 2 * p + h
        masked_go[head] = one_head(go, h)
        delta[head] = jnp.sum(product[h * HEAD : (h + 1) * HEAD], 0, keepdims=True)
        acc[head] = jnp.zeros(acc.shape[1:], F32)

    def visit(blocks, allowed=None):
        found = [read_block(pairs, p, xh, y) for xh, y in blocks]
        turned = [kv[:, :LANES].T for kv in found]
        scores = [[nt(kv[:, :LANES], masked[2 * p + h]) for h in range(2)] for kv in found]
        grads = [[nt(kv[:, LANES:], masked_go[2 * p + h]) for h in range(2)] for kv in found]
        low, low_grads = [], []
        for b in range(2):
            for h in range(2):
                score = scores[b][h]
                if allowed is not None:
                    score = jnp.where(allowed[b], score, -1e30)
                weights = jnp.exp(score - lse[2 * p + h])
                low_grads.append((weights * (grads[b][h] - delta[2 * p + h])).astype(BF))
                low.append(weights.astype(BF))
        for b, (xh, y) in enumerate(blocks):
            grad_keys = grad_values = None
            for h in range(2):
                head = 2 * p + h
                more_values = nn(low[2 * b + h], masked_go[head])
                more_keys = nn(low_grads[2 * b + h], masked[head])
                grad_values = more_values if h == 0 else grad_values + more_values
                grad_keys = more_keys if h == 0 else grad_keys + more_keys
            write_block(pairs, p, xh, y, jnp.concatenate([grad_keys, grad_values], 1).astype(BF))
        for h in range(2):
            head = 2 * p + h
            mixed = acc[head]
            for b in range(2):
                mixed = mixed + nn(turned[b][h * HEAD : (h + 1) * HEAD], low_grads[2 * b + h])
            acc[head] = mixed

    def two(j):
        xh, y = lax.div(j, 2), 2 * lax.rem(j, 2)
        return [(xh, y), (xh, y + 1)]

    odd = lax.rem(chip, 2) == 1
    below = causal(core)
    visit(two(lax.div(chip, 2)), [below | odd, below & odd])
    between(0)

    @pl.loop(0, lax.div(chip, 2))
    def _(j):
        visit(two(j))

    between(1)

    @pl.loop(chip + 1, 8)
    def _(j):
        write_block(
            pairs, p, lax.div(j, 4), lax.rem(j, 4), jnp.zeros((256, 2 * LANES), BF)
        )

    both = jnp.concatenate([acc[2 * p], acc[2 * p + 1]], 0) * 0.125
    dq_ref[:, at] = both.T.astype(BF)


def norm_parts(values):
    centred = values - jnp.mean(values, -1, keepdims=True)
    spread = lax.rsqrt(jnp.mean(centred * centred, -1, keepdims=True) + norm_eps)
    return centred * spread, spread


def norm_back(grad, unit, spread, gain):
    scaled = grad * gain
    return spread * (
        scaled
        - jnp.mean(scaled, -1, keepdims=True)
        - unit * jnp.mean(scaled * unit, -1, keepdims=True)
    )


def mine_of(core, row):
    return jnp.where(core == 0, row[:, :384], row[:, 384:])


def read_attention(wa, inward, outward, table):
    rows = []
    for s in range(8):
        lead = (s // 2, s % 2)
        for j in range(9):
            inward[96 * s : 96 * s + 96, j * LANES : (j + 1) * LANES] = load_rows(
                wa, lead, IN_AT + 96 * j, 96
            )
        for j in range(6):
            outward[96 * s : 96 * s + 96, j * LANES : (j + 1) * LANES] = load_rows(
                wa, lead, OUT_AT + 96 * j, 96
            )
        rows.append(load_rows(wa, lead, VEC_AT, 16).astype(F32)[:, :96])
    table[...] = jnp.concatenate(rows, 1)


def read_hidden(wb, expand, contract):
    for s in range(8):
        lead = (s // 2, s % 2)
        for j in range(12):
            expand[96 * s : 96 * s + 96, j * LANES : (j + 1) * LANES] = load_rows(
                wb, lead, EXP_AT + 96 * j, 96
            )
        for j in range(6):
            contract[192 * s : 192 * s + 192, j * LANES : (j + 1) * LANES] = load_rows(
                wb, lead, CON_AT + 192 * j, 192
            )


def project(core, own, other, inward, table, query, pairs, xh, y, normed):
    tokens = jnp.concatenate([own[0], other[0]], 0).astype(F32)
    unit, _ = norm_parts(tokens)
    low = (unit * table[0:1, :] + table[1:2, :]).astype(BF)
    normed[...] = low
    query[...] = (nn(low, inward[:, :384]) + mine_of(core, table[2:3, :])).astype(BF)
    keys = nn(low, inward[:, 384:768]).astype(BF)
    values = (nn(low, inward[:, 768:]) + mine_of(core, table[3:4, :])).astype(BF)
    for p in range(3):
        at = slice(p * LANES, (p + 1) * LANES)
        write_block(pairs, p, xh, y, jnp.concatenate([keys[:, at], values[:, at]], 1))


def bias_up_of(core, table):
    parts = []
    for s in range(8):
        row = table[8 + s // 2 : 9 + s // 2, :]
        at = 384 * (s % 2)
        parts.append(jnp.where(core == 0, row[:, at : at + 192], row[:, at + 192 : at + 384]))
    return jnp.concatenate(parts, 1)


def out_rows(outward, core):
    return outward[pl.ds(pl.multiple_of(core * 384, 128), 384), :]


def hidden_layer(
    core, own, other, cot, cot_other, attended, attended_other, outward, table, expand, contract,
    middle, result, grad_two, grad_up, turned, active_low, grad_pre_low,
):
    tokens = jnp.concatenate([own[0], other[0]], 0).astype(F32)
    mixed = nn(attended[...], out_rows(outward, core))
    mixed = mixed + nn(attended_other[...], out_rows(outward, 1 - core))
    middle[...] = tokens + mixed + table[4:5, :]
    unit, _ = norm_parts(middle[...])
    low = (unit * table[5:6, :] + table[6:7, :]).astype(BF)
    turned[...] = low.T
    cotangent = jnp.concatenate([cot[0], cot_other[0]], 0)
    bias = bias_up_of(core, table)
    for ch in range(4):
        at = slice(384 * ch, 384 * ch + 384)
        u = nn(low, expand[:, at]) + bias[:, at]
        square = u * u
        bend = jnp.tanh(0.7978845608028654 * u * (1.0 + 0.044715 * square))
        half_up = 0.5 * (1.0 + bend)
        active = (u * half_up).astype(BF)
        slope = half_up + 0.5 * u * (1.0 - bend * bend) * (
            0.7978845608028654 * (1.0 + 0.134145 * square)
        )
        low_result = nn(active, contract[at, :])
        grad_pre = (nt(cotangent, contract[at, :]) * slope).astype(BF)
        low_two = nt(grad_pre, expand[:, at])
        active_low[:, at] = active
        grad_pre_low[:, at] = grad_pre
        if ch == 0:
            result[...] = low_result
            grad_two[...] = low_two
        else:
            result[...] = result[...] + low_result
            grad_two[...] = grad_two[...] + low_two
        grad_up[0:1, at] = jnp.sum(grad_pre.astype(F32), 0, keepdims=True)


def hidden_gradients(cot, cot_other, turned, active_low, grad_pre_low, part):
    cotangent = jnp.concatenate([cot[0], cot_other[0]], 0)
    for ch in range(4):
        at = slice(384 * ch, 384 * ch + 384)
        grad_contract = nn(active_low[:, at].T, cotangent).astype(BF)
        for k in range(2):
            for j in range(6):
                store_rows(
                    part,
                    (ch, k),
                    CON_AT + 192 * j,
                    grad_contract[192 * k : 192 * k + 192, j * LANES : (j + 1) * LANES],
                )
        grad_expand = nn(turned[...], grad_pre_low[:, at]).astype(BF)
        for s in range(8):
            for j in range(3):
                store_rows(
                    part,
                    (s // 2, s % 2),
                    EXP_AT + 96 * (3 * ch + j),
                    grad_expand[96 * s : 96 * s + 96, j * LANES : (j + 1) * LANES],
                )


def branch_back(
    core, cot, cot_other, middle, grad_two, grad_two_other, outward, table,
    grad_middle, grad_attended, grad_branch, rows,
):
    unit, spread = norm_parts(middle[...])
    mine = grad_two[...]
    cotangent = jnp.concatenate([cot[0], cot_other[0]], 0).astype(F32)
    total = cotangent + norm_back(mine + grad_two_other[...], unit, spread, table[5:6, :])
    grad_middle[...] = total
    low = total.astype(BF)
    grad_attended[...] = nt(low, out_rows(outward, core)).astype(BF)
    grad_branch[...] = low
    rows[0:1, :] = jnp.sum(low[:128].astype(F32), 0, keepdims=True)
    rows[1:2, :] = jnp.sum(mine * unit, 0, keepdims=True)
    rows[2:3, :] = jnp.sum(mine, 0, keepdims=True)
    rows[3:4, :] = jnp.sum(cotangent[:128], 0, keepdims=True)


def beside(core, row):
    blank = jnp.zeros_like(row)
    return jnp.where(
        core == 0, jnp.concatenate([row, blank], 1), jnp.concatenate([blank, row], 1)
    )


def store_inward(early, late, index, tile):
    for s in range(8):
        rows = tile[96 * s : 96 * s + 96]
        if index < EARLY:
            store_rows(early, (s // 2, s % 2), 96 * index, rows)
        else:
            store_rows(late, (s // 2, s % 2), 96 * (index - EARLY), rows)


def query_back(
    core, normed, grad_query, inward, attended, grad_branch, turned, early, late, grad_one
):
    turned[...] = normed[...].T
    grad_out = nn(attended[...].T, grad_branch[...]).astype(BF)
    grad = nn(turned[...], grad_query[...]).astype(BF)
    for j in range(3):
        store_inward(early, late, j, grad[:, j * LANES : (j + 1) * LANES])
    none = jnp.zeros((96, LANES), BF)
    for k in range(4):
        for j in range(6):
            store_rows(
                early,
                (2 * core + k // 2, k % 2),
                OUT_EARLY + 96 * j,
                grad_out[96 * k : 96 * k + 96, j * LANES : (j + 1) * LANES],
            )
            store_rows(early, (2 * (1 - core) + k // 2, k % 2), OUT_EARLY + 96 * j, none)
    grad_one[...] = nt(grad_query[...], inward[:, :384])


def pair_back(p, grad_pairs, inward, turned, early, late, grad_one):
    for k in range(2):
        grad = grad_pairs[p, :, k * LANES : (k + 1) * LANES]
        at = 384 + 384 * k + LANES * p
        store_inward(early, late, 3 * k + 3 + p, nn(turned[...], grad).astype(BF))
        grad_one[...] = grad_one[...] + nt(grad, inward[:, at : at + LANES])


def fixed_rows(core, grad_query, rows, grad_up, out):
    out[2:3, :] = beside(core, jnp.sum(grad_query[...].astype(F32), 0, keepdims=True))
    out[4:8, :] = rows[0:4, :]
    ups = [beside(core, grad_up[0:1, 192 * s : 192 * s + 192]) for s in range(8)]
    up = jnp.concatenate(ups, 1)
    for k in range(4):
        out[8 + k : 9 + k, :] = up[:, 768 * k : 768 * k + 768]
    out[12:16, :] = jnp.zeros((4, 768), F32)


def vectors_back(core, own, other, grad_pairs, grad_one, table, late):
    one = grad_one[...]
    tokens = jnp.concatenate([own[0], other[0]], 0).astype(F32)
    unit, _ = norm_parts(tokens)
    values = jnp.concatenate([grad_pairs[p, :, LANES:] for p in range(3)], 1)
    table[0:1, :] = jnp.sum(one * unit, 0, keepdims=True)
    table[1:2, :] = jnp.sum(one, 0, keepdims=True)
    table[3:4, :] = beside(core, jnp.sum(values.astype(F32), 0, keepdims=True))
    side = jnp.zeros((16, LANES - 96), F32)
    for s in range(8):
        tile = jnp.concatenate([table[:, 96 * s : 96 * s + 96], side], 1).astype(BF)
        store_rows(late, (s // 2, s % 2), VEC_LATE, tile)


def blank_rows(late):
    for s in range(8):
        store_rows(late, (s // 2, s % 2), VEC_LATE + 16, jnp.zeros((80, LANES), BF))


def adam_step(weight, moment_one, moment_two, gradient, learn_rate, decay_share):
    first_new = beta_first * moment_one + (1.0 - beta_first) * gradient
    second_new = beta_second * moment_two + (1.0 - beta_second) * gradient * gradient
    first_hat = first_new / (1.0 - beta_first**STEP)
    second_hat = second_new / (1.0 - beta_second**STEP)
    weight_new = weight - learn_rate * (
        first_hat / (jnp.sqrt(second_hat) + adam_eps) + decay_share * weight
    )
    return (first_new, second_new, weight_new)


def update(arrays, index, gradient):
    weight, first, second = arrays
    first[index], second[index], weight[index] = adam_step(
        weight[index], first[index], second[index], gradient.astype(F32), rate_matrix, decay_matrix
    )


def update_inward(early, late, inward, index):
    got, start = (early, 96 * index) if index < EARLY else (late, 96 * (index - EARLY))
    for core in range(2):
        k = index // 3 * 6 + core * 3 + index % 3
        tile = load_rows(got, (core,), start, 96)
        update(inward, (slice(None), slice(k * LANES, (k + 1) * LANES)), tile)


def update_outward(got, outward):
    for j in range(6):
        both = [load_rows(got, (c,), OUT_EARLY + 96 * j, 96).astype(F32) for c in range(2)]
        update(outward, (slice(None), slice(j * LANES, (j + 1) * LANES)), both[0] + both[1])


def update_vectors(got, olds, news):
    both = [load_rows(got, (c,), VEC_LATE, 16).astype(F32) for c in range(2)]
    gradient = (both[0] + both[1])[:12, :96]
    weight, first, second = [old[...] for old in olds]
    new = adam_step(weight, first, second, gradient, rate_vector, 0.0)
    for ref, value in zip((news[1], news[2], news[0]), new):
        ref[...] = value


def update_expand(got, expand, pair):
    wide = [
        jnp.concatenate(
            [load_rows(got, (c,), EXP_AT + 96 * (3 * pair + j), 96) for j in range(3)], 1
        )
        for c in range(2)
    ]
    for k in range(2):
        at = 768 * pair + 384 * k
        tile = jnp.concatenate([w[:, 192 * k : 192 * k + 192] for w in wide], 1)
        update(expand, (slice(None), slice(at, at + 384)), tile)


def update_contract(got, contract, quarter):
    c, h = quarter // 2, quarter % 2
    for j in range(6):
        tile = load_rows(got, (c,), CON_AT + 192 * j + 96 * h, 96)
        rows = slice(96 * quarter, 96 * quarter + 96)
        update(contract, (rows, slice(j * LANES, (j + 1) * LANES)), tile)


class Named:
    def __init__(self, names, refs):
        at = 0
        for name, count in names:
            setattr(self, name, refs[at] if count is None else refs[at : at + count])
            at += 1 if count is None else count


def layer_scratch():
    a, b = GROUP_ROWS
    rows, model, half, hidden, heads = 256, 768, 384, 1536, 6
    named = {
        "inward_f32": pltpu.VMEM((96, 2304), F32),
        "outward_f32": pltpu.VMEM((96, 768), F32),
        "expand_f32": pltpu.VMEM((96, 3072), F32),
        "contract_f32": pltpu.VMEM((384, 768), F32),
        "own_a": pltpu.VMEM((2, 4, a, LANES), BF),
        "own_b": pltpu.VMEM((2, 4, b, LANES), BF),
        "wa": stream_buffers(a),
        "wb": stream_buffers(b),
        "other": pltpu.VMEM((1, 128, model), BF),
        "cot_other": pltpu.VMEM((1, 128, model), BF),
        "inward": pltpu.VMEM((model, 3 * half), BF),
        "outward": pltpu.VMEM((model, model), BF),
        "expand": pltpu.VMEM((model, hidden), BF),
        "contract": pltpu.VMEM((hidden, model), BF),
        "table": pltpu.VMEM((16, model), F32),
        "query": pltpu.VMEM((rows, half), BF),
        "normed": pltpu.VMEM((rows, model), BF),
        "pairs": [
            pltpu.VMEM((3, 4, 2, KV_ROWS[0][1], 2 * LANES), BF),
            pltpu.VMEM((3, 2, 4, KV_ROWS[1][1], 2 * LANES), BF),
        ],
        "pass_x": [pltpu.VMEM((KV_ROWS[0][1] // 2, 2 * LANES), BF)] * 6,
        "pass_y": [pltpu.VMEM((2, KV_ROWS[1][1], 2 * LANES), BF)] * 6,
        "masked": pltpu.VMEM((heads, rows, LANES), BF),
        "masked_go": pltpu.VMEM((heads, rows, LANES), BF),
        "top": pltpu.VMEM((heads, 1, rows), F32),
        "mass": pltpu.VMEM((heads, 1, rows), F32),
        "acc": pltpu.VMEM((heads, HEAD, rows), F32),
        "attended": pltpu.VMEM((rows, half), F32),
        "attended_low": pltpu.VMEM((rows, half), BF),
        "attended_other": pltpu.VMEM((rows, half), BF),
        "middle": pltpu.VMEM((rows, model), F32),
        "result": pltpu.VMEM((rows, model), F32),
        "result_other": pltpu.VMEM((128, model), F32),
        "grad_two": pltpu.VMEM((rows, model), F32),
        "grad_two_other": pltpu.VMEM((rows, model), F32),
        "grad_up": pltpu.VMEM((8, hidden), F32),
        "grad_middle": pltpu.VMEM((rows, model), F32),
        "grad_attended": pltpu.VMEM((rows, half), BF),
        "grad_branch": pltpu.VMEM((rows, model), BF),
        "grad_rows": pltpu.VMEM((8, model), F32),
        "grad_table": pltpu.VMEM((16, model), F32),
        "grad_query": pltpu.VMEM((rows, half), BF),
        "grad_pairs": pltpu.VMEM((3, rows, 2 * LANES), BF),
        "grad_one": pltpu.VMEM((rows, model), F32),
        "grad_one_other": pltpu.VMEM((128, model), F32),
        "pairs_a": pairs_scratch(2 * LANES)[0] * 3,
        "pairs_b": pairs_scratch(2 * LANES)[1] * 3,
        "turned": pltpu.VMEM((model, rows), BF),
        "active_low": pltpu.VMEM((rows, hidden), BF),
        "grad_pre_low": pltpu.VMEM((rows, hidden), BF),
        "early": stream_buffers(PART_ROWS),
        "late": stream_buffers(PART_ROWS),
        "flow_early": sum_scratch(PART_ROWS, True),
        "flow_late": sum_scratch(PART_ROWS, False),
        "flow_b": sum_scratch(b, True),
        "send": pltpu.SemaphoreType.DMA((SLOTS,)),
        "recv": pltpu.SemaphoreType.DMA((SLOTS,)),
        "local": pltpu.SemaphoreType.DMA((10,)),
    }
    names, shapes = [], []
    for name, value in named.items():
        several = isinstance(value, list)
        names.append((name, len(value) if several else None))
        shapes += value if several else [value]
    return names, shapes


SLOTS = 6 * 12 + 3 * 20 + 3 * 20 + 2 * (3 * 12 + 8) + 27 + 15 + 10


def layer_kernel(
    tokens, cot, inward, outward, expand, contract, table,
    layer, input_grad, got_b, got_early, got_late, *scratch,
):
    m = Named(layer_scratch()[0], scratch)
    place = Place()
    core, sibling = place.core, place.sibling()
    xh, y = lax.div(place.at[0], 2), place.at[1]
    chip = xh * 4 + y

    others = [place.along(axis, by) for axis in range(3) for by in (1, 2, 3)]
    others += [place.of_sequence(2, by) for by in (1, 2, 3)]
    others += [place.of_sequence(bx, by, 1) for bx in (0, 2) for by in range(4)]
    greet(others)
    loads = [
        pltpu.make_async_copy(src, dst, m.local.at[n])
        for n, (src, dst) in enumerate(
            (
                (inward, m.inward_f32),
                (outward, m.outward_f32),
                (expand, m.expand_f32),
                (contract, m.contract_f32),
            )
        )
    ]
    for load in loads:
        load.start()

    def lay_out(own, out, slot):
        copies = [
            pltpu.make_async_copy(
                own.at[xh, y, stream_rows(own.shape[-2], s)],
                pieces(out, s, (), place.at),
                m.local.at[slot + s],
            )
            for s in range(3)
        ]
        for copy in copies:
            copy.start()
        for copy in copies:
            copy.wait()

    links = Links(m.send, m.recv)

    def send_over(links, *moves):
        slots = links.take(len(moves))
        for (src, dst), slot in zip(moves, slots):
            links.start(src, dst, slot, sibling)
        return [(dst, slot) for (_, dst), slot in zip(moves, slots)]

    def wait_over(links, waits):
        for dst, slot in waits:
            links.arrived(dst, slot, sibling)

    def changed_over(src, dst):
        low, high = pl.ds(0, 128), pl.ds(128, 128)
        return (src.at[low], dst.at[high]), (src.at[high], dst.at[low])

    loads[0].wait()
    loads[1].wait()
    pack_attention(core, m.inward_f32, m.outward_f32, table, m.own_a)
    lay_out(m.own_a, m.wa, 4)
    meet(others)

    gather_a, gather_b = links.branch(), links.branch()
    flows_a = [gather_flow(gather_a, place, m.wa, s) for s in range(3)]
    flows_b = [gather_flow(gather_b, place, m.wb, s) for s in range(3)]
    step(flows_a)
    waits = send_over(links, (tokens, m.other), (cot, m.cot_other))
    loads[2].wait()
    loads[3].wait()
    pack_hidden(core, m.expand_f32, m.contract_f32, m.own_b)
    lay_out(m.own_b, m.wb, 7)
    for _ in range(2):
        step(flows_b)
        step(flows_a)
    in_step(flows_a)
    step(flows_b)
    read_attention(m.wa, m.inward, m.outward, m.table)
    wait_over(links, waits)
    project(
        core, tokens, m.other, m.inward, m.table, m.query, m.pairs, xh, y, m.normed
    )
    gather_kv = links.branch()
    kv = [
        [
            gather_pairs_flow(
                gather_kv, place, m.pairs[group].at[p], group,
                *(m.pass_x, m.pass_y)[group][2 * p : 2 * p + 2],
            )
            for group in range(2)
        ]
        for p in range(3)
    ]
    step(kv[0])
    masked_heads(m.query, m.masked)
    state = (m.masked, m.top, m.mass, m.acc)
    allowed = causal(core)
    for p in range(3):
        attend_blocks(p, [read_block(m.pairs, p, xh, y)], allowed, *state)
        for q in range(p + 1):
            step(kv[q])
        if p < 2:
            step(kv[p + 1])
    in_step(kv[0])
    step(flows_b)
    for p in range(3):

        def visit(blocks, p=p):
            attend_blocks(p, [read_block(m.pairs, p, bx, by) for bx, by in blocks], None, *state)

        def steps(k, p=p):
            for q in range(p + 1, 3):
                step(kv[q])

        earlier_blocks(chip, visit, steps)
        attend_end(p, m.attended, m.attended_low, m.top, m.mass, m.acc)
        if p < 2:
            in_step(kv[p + 1])
    waits = send_over(links, *changed_over(m.attended_low, m.attended_other))
    in_step(flows_b)
    read_hidden(m.wb, m.expand, m.contract)
    gather_a.close()
    gather_b.close()
    gather_kv.close()
    wait_over(links, waits)
    hidden_layer(
        core, tokens, m.other, cot, m.cot_other, m.attended_low, m.attended_other, m.outward,
        m.table, m.expand, m.contract, m.middle, m.result, m.grad_two, m.grad_up, m.turned,
        m.active_low, m.grad_pre_low,
    )

    waits = send_over(links, *changed_over(m.grad_two, m.grad_two_other))
    hidden_gradients(cot, m.cot_other, m.turned, m.active_low, m.grad_pre_low, m.wb)
    reduce_b, reduce_kv = links.branch(), links.branch()
    reduce_early, reduce_late = links.branch(), links.branch()

    flows_b = [group_flow(reduce_b, place, m.wb, got_b, m.flow_b, True, False)]
    step(flows_b)
    result_waits = send_over(links, (m.result.at[pl.ds(128, 128)], m.result_other))
    wait_over(links, waits)
    branch_back(
        core, cot, m.cot_other, m.middle, m.grad_two, m.grad_two_other, m.outward, m.table,
        m.grad_middle, m.grad_attended, m.grad_branch, m.grad_rows,
    )
    reduce_pairs = [
        [
            reduce_pairs_flow(
                reduce_kv, place, m.pairs[group].at[p], m.grad_pairs.at[p], group,
                (m.pairs_a, m.pairs_b)[group][8 * p : 8 * p + 8],
            )
            for group in range(2)
        ]
        for p in range(3)
    ]
    for p in range(3):

        def steps(k, p=p):
            for q in range(p):
                step(reduce_pairs[q])
            if (p, k) == (1, 0):
                step(flows_b)

        attend_back(
            p, chip, core, m.pairs, m.attended, m.grad_attended, m.top, m.grad_query,
            m.masked, m.masked_go, m.mass, m.acc, steps,
        )
        step(reduce_pairs[p])
    for flows in reduce_pairs:
        step(flows)
    query_back(
        core, m.normed, m.grad_query, m.inward, m.attended_low, m.grad_branch, m.turned, m.early,
        m.late, m.grad_one,
    )
    flows_early = [group_flow(reduce_early, place, m.early, got_early, m.flow_early, True, False)]
    step(flows_early)
    wait_over(links, result_waits)
    layer[0] = (
        m.middle[0:128, :] + (m.result[0:128, :] + m.result_other[...]) + m.table[7:8, :]
    ).astype(BF)
    fixed_rows(core, m.grad_query, m.grad_rows, m.grad_up, m.grad_table)
    blank_rows(m.late)
    for p in range(3):
        while reduce_pairs[p]:
            for flows in reduce_pairs[p:]:
                step(flows)
            if p == 2:
                step(flows_b)
            step(flows_early)
        pair_back(p, m.grad_pairs, m.inward, m.turned, m.early, m.late, m.grad_one)
    vectors_back(core, tokens, m.other, m.grad_pairs, m.grad_one, m.grad_table, m.late)
    flows_late = [group_flow(reduce_late, place, m.late, got_late, m.flow_late, False, True)]
    step(flows_late)
    waits = send_over(links, (m.grad_one.at[pl.ds(128, 128)], m.grad_one_other))
    for _ in range(2):
        step(flows_b)
        step(flows_early)
        step(flows_late)
    wait_over(links, waits)
    unit, spread = norm_parts(tokens[0].astype(F32))
    grad = m.grad_one[0:128, :] + m.grad_one_other[...]
    input_grad[0] = m.grad_middle[0:128, :] + norm_back(grad, unit, spread, m.table[0:1, :])
    while flows_b or flows_early or flows_late:
        step(flows_b)
        step(flows_early)
        step(flows_late)
    for each in (links, reduce_b, reduce_kv, reduce_early, reduce_late):
        each.close()


def update_kernel(layer_in, grad_in, got_b, got_early, got_late, *refs):
    olds = [[refs[k], refs[5 + k], refs[10 + k]] for k in range(5)]
    layer, input_grad = refs[15:17]
    news = [[refs[19 + 3 * k], refs[17 + 3 * k], refs[18 + 3 * k]] for k in range(5)]
    buffers = [refs[32 + 3 * k : 35 + 3 * k] for k in range(4)]
    sums_b, sums_early, sums_late, layer_held, grad_held = refs[44:49]
    sem = refs[49]
    used = []

    def copies(*moves, priority=0):
        made = []
        for src, dst in moves:
            copy = pltpu.make_async_copy(src, dst, sem.at[len(used)])
            copy.start(priority=priority)
            used.append(copy)
            made.append(copy)
        return made

    def wait(made):
        for copy in made:
            copy.wait()

    every = slice(None)
    first = copies((got_b, sums_b))
    chunks = [
        (2, (every, pl.ds(768 * k, 768)), partial(update_expand, sums_b, buffers[2], k))
        for k in range(4)
    ]
    chunks += [
        (3, (pl.ds(96 * k, 96), every), partial(update_contract, sums_b, buffers[3], k))
        for k in range(4)
    ]
    chunks.append((1, (every, every), partial(update_outward, sums_early, buffers[1])))

    def part(k):
        for index in range(3 * k, 3 * k + 3):
            update_inward(sums_early, sums_late, buffers[0], index)

    chunks += [(0, (every, pl.ds(768 * k, 768)), partial(part, k)) for k in range(3)]

    def load(chunk):
        n, at, _ = chunk
        return copies(*[(old.at[at], buffer.at[at]) for old, buffer in zip(olds[n], buffers[n])])

    ahead = 3
    loads = [load(chunk) for chunk in chunks[:ahead]]
    last = copies((got_early, sums_early), (got_late, sums_late))
    done = copies((layer_in, layer_held), (grad_in, grad_held))
    out = []
    wait(first)
    for k, (n, at, compute) in enumerate(chunks):
        wait(loads[k])
        if k == 8:
            wait(last + done)
            out += copies((layer_held, layer), (grad_held, input_grad))
            update_vectors(sums_late, olds[4], news[4])
        if k + ahead < len(chunks):
            loads.append(load(chunks[k + ahead]))
        compute()
        moves = [(buffer.at[at], new.at[at]) for buffer, new in zip(buffers[n], news[n])]
        out += copies(*moves, priority=1)
    wait(out)


def on_device(inputs, cotangent, *state):
    b = GROUP_ROWS[1]
    vmem = pl.BlockSpec(memory_space=pltpu.VMEM)
    ref = pl.BlockSpec(memory_space=pl.ANY)
    shapes = (
        jax.ShapeDtypeStruct(inputs.shape, BF),
        jax.ShapeDtypeStruct(inputs.shape, F32),
        jax.ShapeDtypeStruct((2, 2, 4, b, LANES), BF),
        jax.ShapeDtypeStruct((2, 2, 4, PART_ROWS, LANES), BF),
        jax.ShapeDtypeStruct((2, 2, 4, PART_ROWS, LANES), BF),
    )
    made = pl.pallas_call(
        layer_kernel,
        out_shape=shapes,
        in_specs=[vmem, vmem] + [ref] * 4 + [vmem],
        out_specs=tuple([vmem] * 5),
        scratch_shapes=layer_scratch()[1],
        compiler_params=pltpu.CompilerParams(
            collective_id=0, has_side_effects=True, vmem_limit_bytes=60 * MIB
        ),
        name="layer",
    )(inputs, cotangent, *state[:5])
    return pl.pallas_call(
        update_kernel,
        out_shape=(
            *shapes[:2],
            *[jax.ShapeDtypeStruct(w.shape, F32) for w in state[:5] for _ in range(3)],
        ),
        in_specs=[ref] * 5 + ([ref] * 4 + [vmem]) * 3,
        out_specs=tuple([ref] * 14 + [vmem] * 3),
        scratch_shapes=[
            *[pltpu.VMEM(w.shape, F32) for w in state[:4] for _ in range(3)],
            *[pltpu.VMEM(s.shape, BF) for s in shapes[2:]],
            *[pltpu.VMEM(s.shape, s.dtype) for s in shapes[:2]],
            pltpu.SemaphoreType.DMA((84,)),
        ],
        compiler_params=pltpu.CompilerParams(vmem_limit_bytes=60 * MIB),
        name="update",
    )(*made, *state)


def solution(mesh):
    tokens = P("shard", "ctx", None)
    matrix = P("shard", None)
    table = P(None, "shard")
    in_specs = (tokens, tokens) + (matrix, matrix, matrix, matrix, table) * 3
    out_specs = (tokens, tokens) + (matrix,) * 12 + (table,) * 3
    return jax.shard_map(
        on_device, mesh=mesh, in_specs=in_specs, out_specs=out_specs, check_vma=False
    )
```
